32 devices in a mesh: row: 8 (over z, y), col: 4 (over x, core).
Axes of the slice: x: 2, y: 2, z: 4, core: 2. Of those that a mesh axis runs over, the one named last changes fastest.
Arguments:
- gradients: bfloat16 [2, 32768, 16384], P(None, 'row', 'col'), may hold values from -17 to 17
- sketch_matrix: bfloat16 [16384, 256], P('col'), may hold values from -0.046875 to 0.046875
Outputs:
- projector: bfloat16 [2, 32768, 256], P(None, ('row', 'col'))
- projected: float32 [256, 2, 16384], P('row', None, 'col')
The draws below stay inside these ranges and needn't reach their ends.
All inputs are finite; a program needn't handle non-finite values.
Results may differ from the reference program's by a relative error of at most 0.01.
Values may be sent and summed in bfloat16 or wider, within the bound.
A program may use at most 192 MiB of HBM per device.

```python
import math
import jax
import jax.numpy as jnp
from jax import lax

D = 16384
FF = 32768
K = 256


def draw_gradients(key, part):
    key = jax.random.fold_in(key, 7)
    subkeys = jax.random.split(key, 2)
    position = (jnp.arange(FF, dtype=jnp.float32) + 0.5) / FF
    spread = 10.0 ** jax.random.uniform(subkeys[1], (2, FF, 1), jnp.float32, -0.5, 0.5)
    entries = jax.random.truncated_normal(subkeys[0], -4.0, 4.0, (2, FF, D), jnp.float32)
    ramp_rows = (1.0 + 2.0 * position) / 3.0
    return (entries * spread * ramp_rows[None, :, None]).astype(jnp.bfloat16)


def shard_levels(stream_key, shape, cuts, smallest, largest):
    factor_of, own = 1.0, jax.random.fold_in(stream_key, 6)
    for dim, shards_of in cuts:
        heights = jnp.exp(jax.random.uniform(jax.random.fold_in(own, dim), (shards_of,), jnp.float32, smallest / len(cuts), largest / len(cuts)))
        factor_of = factor_of * jnp.repeat(heights, shape[dim] // shards_of).reshape([-1 if axis == dim else 1 for axis in range(len(shape))])
    return factor_of


def scatter_about(own_key, shape, deviation, limit, pieces=(), kind=jnp.bfloat16):
    drawn = deviation * jax.random.normal(own_key, shape, jnp.float32)
    if pieces:
        drawn = drawn * shard_levels(own_key, shape, pieces, -0.22, 0.18)
    return jnp.clip(drawn, -limit, limit).astype(kind)


def setup_inputs(seed: int = 0) -> dict:
    streams_of = jax.random.split(jax.random.key(seed), 3)
    return {
        "gradients": draw_gradients(jax.random.fold_in(streams_of[2], 71), 0),
        "sketch_matrix": scatter_about(streams_of[1], (D, K), D ** -0.5, 0.046875, ((0, 4),)),
    }


def invert_low(factor_low):
    identity = jnp.eye(factor_low.shape[-1], dtype=jnp.float32)
    return jax.scipy.linalg.solve_triangular(factor_low, identity, lower=True)

def reference(gradients, sketch_matrix):
    projectors = []
    projections = []
    for matrix_id in range(2):
        grad_rows = gradients[matrix_id]
        sketch_rows = jnp.dot(grad_rows.astype(jnp.float32), sketch_matrix.astype(jnp.float32), preferred_element_type=jnp.float32).astype(jnp.bfloat16)
        gram_mean = jnp.dot(sketch_rows.T.astype(jnp.float32), sketch_rows.astype(jnp.float32), preferred_element_type=jnp.float32) / FF
        factor_low = jnp.linalg.cholesky(gram_mean)
        inverse_low = invert_low(factor_low)
        basis = jnp.dot(sketch_rows.astype(jnp.float32), inverse_low.T, precision=lax.Precision.HIGHEST)
        projectors.append(basis.astype(jnp.bfloat16))
        moment = jnp.dot(sketch_rows.T.astype(jnp.float32), grad_rows.astype(jnp.float32), preferred_element_type=jnp.float32)
        projections.append(jnp.dot(inverse_low, moment, precision=lax.Precision.HIGHEST) * (1.0 / math.sqrt(FF)))
    return (jnp.stack(projectors, 0), jnp.stack(projections, 1))
```

```python
import functools
import math

import jax
import jax.numpy as jnp
from jax import lax
from jax.experimental import pallas as pl
from jax.experimental.pallas import tpu as pltpu
from jax.sharding import PartitionSpec as P

HIGHEST = lax.Precision.HIGHEST


def factor_inverse_kernel(scale, block, gram_ref, inverse_ref, work):
    count, rank, _ = gram_ref.shape
    lanes = lax.broadcasted_iota(jnp.int32, (rank, rank), 1)
    rows = lax.broadcasted_iota(jnp.int32, (rank, rank), 0)
    for m in range(count):
        work[m, :, :rank] = gram_ref[m] * scale
        work[m, :, rank:] = jnp.where(lanes == rows, 1.0, 0.0).astype(jnp.float32)
    small_rows = lax.broadcasted_iota(jnp.int32, (block, 2 * block), 0)
    small_lanes = lax.broadcasted_iota(jnp.int32, (block, 2 * block), 1)
    identity = jnp.where(small_rows + block == small_lanes, 1.0, 0.0).astype(jnp.float32)[:, block:]
    for step in range(rank // block):
        low = step * block
        heads = [
            jnp.concatenate([work[m, low : low + block, low : low + block], identity], axis=1)
            for m in range(count)
        ]
        scales = [jnp.zeros((block, 2 * block), jnp.float32) for _ in range(count)]
        for j in range(block):
            for m in range(count):
                head = heads[m]
                column = jnp.broadcast_to(head[:, j : j + 1], head.shape)
                pivot = column[j : j + 1, :]
                row = head[j : j + 1, :]
                ratio = row / pivot
                heads[m] = head - jnp.where(small_rows > j, column, 0.0) * ratio
                scales[m] = jnp.where(small_rows == j, lax.rsqrt(pivot), scales[m])
        for m in range(count):
            corner = (heads[m] * scales[m])[:, block:]
            panel = jnp.dot(corner, work[m, low : low + block, :], precision=HIGHEST, preferred_element_type=jnp.float32)
            work[m, low : low + block, :] = panel
            if low + block < rank:
                work[m, low + block :, :] -= lax.dot_general(
                    panel[:, low + block : rank], panel, (((0,), (0,)), ((), ())),
                    precision=HIGHEST, preferred_element_type=jnp.float32,
                )
    for m in range(count):
        inverse_ref[m] = jnp.where(lanes <= rows, work[m, :, rank:], 0.0)


def factor_inverse(gram_sum, total_rows):
    count, rank, _ = gram_sum.shape
    return pl.pallas_call(
        functools.partial(factor_inverse_kernel, 1.0 / total_rows, 32),
        out_shape=jax.ShapeDtypeStruct(gram_sum.shape, jnp.float32),
        in_specs=[pl.BlockSpec(memory_space=pltpu.VMEM)],
        out_specs=pl.BlockSpec(memory_space=pltpu.VMEM),
        scratch_shapes=[pltpu.VMEM((count, rank, 2 * rank), jnp.float32)],
        compiler_params=pltpu.CompilerParams(vmem_limit_bytes=16 << 20),
        cost_estimate=pl.CostEstimate(flops=20_000_000_000, bytes_accessed=2 << 20, transcendentals=0),
    )(gram_sum)


MESH = pl.DeviceIdType.MESH
SLOTS = 7
BLOCK = 256
TILE = 1024


def remote(source, target, send_sem, recv_sem, device):
    return pltpu.make_async_remote_copy(
        src_ref=source, dst_ref=target, send_sem=send_sem, recv_sem=recv_sem,
        device_id=device, device_id_type=MESH,
    )


def range_kernel(
    which, omega_ref, grad_ref, own_ref, gram_ref, keep_ref, give_ref, ring, total, parts,
    send_core, recv_core, send_chip, recv_chip, sums, grad_sem, send_sems, recv_sems,
):
    blocks = sums.shape[0]
    half_rows, rank = sums.shape[2:]
    row, col = lax.axis_index("row"), lax.axis_index("col")
    core = lax.rem(col, 2)
    sibling = (row, col + 1 - 2 * core)
    across = (row, lax.rem(col + 2, 4))

    def fetch(b):
        return pltpu.make_async_copy(
            grad_ref.at[which, pl.ds(b * BLOCK, BLOCK), :], ring.at[lax.rem(b, SLOTS)],
            grad_sem.at[lax.rem(b, SLOTS)],
        )

    def copy_partial(b):
        return remote(send_core.at[b], recv_core.at[b], send_sems.at[0, b], recv_sems.at[0, b], sibling)

    def copy_chip(b):
        return remote(send_chip.at[b], recv_chip.at[b], send_sems.at[1, b], recv_sems.at[1, b], across)

    def copy_sum(b):
        return remote(sums.at[b, core], sums.at[b, core], send_sems.at[2, b], recv_sems.at[2, b], sibling)

    for b in range(SLOTS):
        fetch(b).start()
    barrier = pltpu.get_barrier_semaphore()
    for peer in (sibling, across):
        pl.semaphore_signal(barrier, inc=1, device_id=peer, device_id_type=MESH)
    total[...] = jnp.zeros_like(total)
    gram_ref[...] = jnp.zeros_like(gram_ref)
    pl.semaphore_wait(barrier, 2)

    def step(s, carry):
        @pl.when(s < blocks)
        def _():
            fetch(s).wait()
            partial = jnp.dot(ring[lax.rem(s, SLOTS)], omega_ref[...], preferred_element_type=jnp.float32)
            parts[lax.rem(s, 2)] = partial.reshape(2, half_rows, rank)
            send_core[s] = parts[lax.rem(s, 2), 1 - core].astype(jnp.bfloat16)
            copy_partial(s).start()

        @pl.when((s >= 1) & (s < blocks + 1))
        def _():
            b = s - 1
            copy_partial(b).wait_recv()
            send_chip[b] = (parts[lax.rem(b, 2), core] + recv_core[b].astype(jnp.float32)).astype(jnp.bfloat16)
            copy_chip(b).start()

        @pl.when((s >= 3) & (s < blocks + 3))
        def _():
            b = s - 3
            copy_chip(b).wait_recv()
            sums[b, core] = (send_chip[b].astype(jnp.float32) + recv_chip[b].astype(jnp.float32)).astype(jnp.bfloat16)
            copy_sum(b).start()

        @pl.when(s >= 4)
        def _():
            b = s - 4
            copy_sum(b).wait_recv()
            block = sums[b].reshape(BLOCK, rank)
            turned = block.astype(jnp.float32).T.astype(jnp.bfloat16)
            gram_ref[...] += jnp.dot(turned, block, preferred_element_type=jnp.float32)
            slot = lax.rem(b, SLOTS)
            for low in range(0, total.shape[1], TILE):
                total[:, low : low + TILE] += jnp.dot(
                    turned, ring[slot, :, low : low + TILE], preferred_element_type=jnp.float32
                )

            @pl.when(b + SLOTS < blocks)
            def _():
                fetch(b + SLOTS).start()

        return carry

    lax.fori_loop(0, blocks + 4, step, 0)
    pairs, _, share = keep_ref.shape
    low = lax.rem(row, 2)
    for k in range(pairs):
        pair = 2 * lax.rem(row // 2 + k, pairs)
        keep_ref[k] = total[:, pl.ds(pl.multiple_of((pair + low) * share, share), share)].astype(jnp.bfloat16)
        give_ref[k] = total[:, pl.ds(pl.multiple_of((pair + 1 - low) * share, share), share)].astype(jnp.bfloat16)
    own = own_ref.shape[0]
    for i in range(own):
        own_ref[i] = sums[col * own + i].reshape(BLOCK, rank)

    def finish(b, carry):
        copy_partial(b).wait_send()
        copy_chip(b).wait_send()
        copy_sum(b).wait_send()
        return carry

    lax.fori_loop(0, blocks, finish, 0)


def sketch_and_moment(which, gradients, sketch_matrix, devices):
    _, rows, width = gradients.shape
    rank = sketch_matrix.shape[1]
    blocks = rows // BLOCK
    half = (blocks, BLOCK // 2, rank)
    vmem = pl.BlockSpec(memory_space=pltpu.VMEM)
    moment_half = jax.ShapeDtypeStruct((devices // 2, rank, width // devices), jnp.bfloat16)
    own, gram, keep, give = pl.pallas_call(
        functools.partial(range_kernel, which),
        out_shape=(
            jax.ShapeDtypeStruct((blocks // 4, BLOCK, rank), jnp.bfloat16),
            jax.ShapeDtypeStruct((rank, rank), jnp.float32),
            moment_half,
            moment_half,
        ),
        in_specs=[vmem, pl.BlockSpec(memory_space=pl.ANY)],
        out_specs=(vmem, vmem, vmem, vmem),
        scratch_shapes=[
            pltpu.VMEM((SLOTS, BLOCK, width), jnp.bfloat16),
            pltpu.VMEM((rank, width), jnp.float32),
            pltpu.VMEM((2, 2, BLOCK // 2, rank), jnp.float32),
            pltpu.VMEM(half, jnp.bfloat16),
            pltpu.VMEM(half, jnp.bfloat16),
            pltpu.VMEM(half, jnp.bfloat16),
            pltpu.VMEM(half, jnp.bfloat16),
            pltpu.VMEM((blocks, 2, BLOCK // 2, rank), jnp.bfloat16),
            pltpu.SemaphoreType.DMA((SLOTS,)),
            pltpu.SemaphoreType.DMA((3, blocks)),
            pltpu.SemaphoreType.DMA((3, blocks)),
        ],
        compiler_params=pltpu.CompilerParams(
            collective_id=which, has_side_effects=True, vmem_limit_bytes=44 << 20
        ),
        cost_estimate=pl.CostEstimate(
            flops=4 * rows * width * rank, bytes_accessed=2 * rows * width, transcendentals=0
        ),
    )(sketch_matrix, gradients)
    return own.reshape(rows // 4, rank), gram, keep, give


def gram_kernel(gram_ref, sum_ref, landed, row_send, row_recv, out_send, out_recv, col_send, col_recv):
    count, piece, _ = landed.shape
    row, col = lax.axis_index("row"), lax.axis_index("col")
    cols = lax.axis_size("col")
    quarter = count * piece
    base = col * quarter
    rows_of = lambda r: pl.ds(pl.multiple_of(base + r * piece, piece), piece)
    row_peers = [(lax.rem(row + k, count), col) for k in range(1, count)]
    col_peers = [(row, lax.rem(col + k, cols)) for k in range(1, cols)]
    barrier = pltpu.get_barrier_semaphore()
    for peer in row_peers + col_peers:
        pl.semaphore_signal(barrier, inc=1, device_id=peer, device_id_type=MESH)
    pl.semaphore_wait(barrier, count + cols - 2)

    first = [
        remote(gram_ref.at[rows_of(peer[0])], landed.at[k], row_send.at[k], row_recv.at[k], peer)
        for k, peer in enumerate(row_peers)
    ]
    for copy in first:
        copy.start()
    here = gram_ref[rows_of(row)]
    for k, copy in enumerate(first):
        copy.wait_recv()
        here += landed[k]
    sum_ref[rows_of(row)] = here
    second = [
        remote(sum_ref.at[rows_of(row)], sum_ref.at[rows_of(row)], out_send.at[k], out_recv.at[k], peer)
        for k, peer in enumerate(row_peers)
    ]
    for copy in second:
        copy.start()
    for copy in second:
        copy.wait_recv()
    mine = pl.ds(pl.multiple_of(base, quarter), quarter)
    third = [
        remote(sum_ref.at[mine], sum_ref.at[mine], col_send.at[k], col_recv.at[k], peer)
        for k, peer in enumerate(col_peers)
    ]
    for copy in third:
        copy.start()
    for copy in third:
        copy.wait_recv()
    for copy in first + second + third:
        copy.wait_send()


def add_grams(gram, rows, cols):
    lines, rank = gram.shape
    piece = lines // (rows * cols)
    vmem = pl.BlockSpec(memory_space=pltpu.VMEM)
    return pl.pallas_call(
        gram_kernel,
        out_shape=jax.ShapeDtypeStruct(gram.shape, jnp.float32),
        in_specs=[vmem],
        out_specs=vmem,
        scratch_shapes=[pltpu.VMEM((rows, piece, rank), jnp.float32)]
        + [pltpu.SemaphoreType.DMA((rows - 1,))] * 4
        + [pltpu.SemaphoreType.DMA((cols - 1,))] * 2,
        compiler_params=pltpu.CompilerParams(
            collective_id=2, has_side_effects=True, vmem_limit_bytes=8 << 20
        ),
        cost_estimate=pl.CostEstimate(flops=20_000_000_000, bytes_accessed=2 << 20, transcendentals=0),
    )(gram)


def finish_outputs(mine, gram_sum, moments, total_rows):
    inverse_low = factor_inverse(gram_sum, total_rows)
    inverse_low, moments = lax.optimization_barrier((inverse_low, moments))
    projector = jnp.einsum(
        "mrk,mlk->mrl", mine.astype(jnp.float32), inverse_low, precision=HIGHEST
    ).astype(jnp.bfloat16)
    scaled = inverse_low * (1.0 / math.sqrt(total_rows))
    part = jnp.stack(
        [jnp.dot(scaled[m], moments[m].astype(jnp.float32), precision=HIGHEST) for m in range(2)], 1
    ).astype(jnp.bfloat16)
    projected = lax.all_to_all(part, "row", split_axis=0, concat_axis=2, tiled=True).astype(jnp.float32)
    return (projector, projected)


def add_pairs(keep, give, devices):
    got = lax.ppermute(give, "row", [(r, r + 1 - 2 * (r % 2)) for r in range(devices)])
    paired = keep.astype(jnp.float32) + got.astype(jnp.float32)
    return paired[0], [paired[k].astype(jnp.bfloat16) for k in range(1, devices // 2)]


def add_moments(first, others, devices):
    moment = first
    for k, other in enumerate(others, 1):
        ring = [(r, (r + 2 * k) % devices) for r in range(devices)]
        moment += lax.ppermute(other, "row", ring).astype(jnp.float32)
    return moment


def body_fused(gradients, sketch_matrix):
    rows, cols = lax.axis_size("row"), lax.axis_size("col")
    mine, grams, pairs = [], [], []
    for m in range(2):
        own, gram, keep, give = sketch_and_moment(m, gradients, sketch_matrix, rows)
        mine.append(own)
        grams.append(gram)
        pairs.append(add_pairs(keep, give, rows))
    rank = sketch_matrix.shape[1]
    grams, pairs[0] = lax.optimization_barrier((grams, pairs[0]))
    moment = add_moments(*pairs[0], rows)
    gram_sum = add_grams(jnp.concatenate(grams, 0), rows, cols)
    gram_sum, moment, pairs[1] = lax.optimization_barrier((gram_sum, moment, pairs[1]))
    moments = [moment, add_moments(*pairs[1], rows)]
    return finish_outputs(jnp.stack(mine), gram_sum.reshape(2, rank, rank), moments, gradients.shape[1] * rows)


def body_plain(gradients, sketch_matrix):
    total_rows = gradients.shape[1] * lax.axis_size("row")
    partial_sketch = jnp.einsum(
        "mrd,dk->mrk", gradients, sketch_matrix, preferred_element_type=jnp.float32
    ).astype(jnp.bfloat16)
    mine = lax.psum_scatter(partial_sketch, "col", scatter_dimension=1, tiled=True)
    sketch_rows = lax.all_gather(mine, "col", axis=1, tiled=True)
    local_gram = jnp.einsum("mrk,mrl->mkl", mine, mine, preferred_element_type=jnp.float32)
    gram_sum = lax.psum(local_gram, ("row", "col"))
    moments = []
    for m in range(2):
        moment = jnp.einsum("rk,rd->kd", sketch_rows[m], gradients[m], preferred_element_type=jnp.float32)
        moments.append(lax.psum_scatter(moment.astype(jnp.bfloat16), "row", scatter_dimension=1, tiled=True))
    return finish_outputs(mine, gram_sum, moments, total_rows)


def solution(mesh):
    in_specs = (P(None, "row", "col"), P("col", None))
    out_specs = (P(None, ("row", "col"), None), P("row", None, "col"))

    def body(gradients, sketch_matrix):
        _, rows, width = gradients.shape
        rank = sketch_matrix.shape[1]
        fits = mesh.shape["col"] == 4 and mesh.shape["row"] % 2 == 0 and rows % (4 * BLOCK) == 0 and rows >= SLOTS * BLOCK and width % TILE == 0 and width % (128 * mesh.shape["row"]) == 0
        fits = fits and (2 * rank) % (16 * mesh.shape["row"] * mesh.shape["col"]) == 0
        return (body_fused if fits else body_plain)(gradients, sketch_matrix)

    return jax.shard_map(body, mesh=mesh, in_specs=in_specs, out_specs=out_specs, check_vma=False)
```

```python
import functools
import math

import jax
import jax.numpy as jnp
from jax import lax
from jax.experimental import pallas as pl
from jax.experimental.pallas import tpu as pltpu
from jax.sharding import PartitionSpec as P

HIGHEST = lax.Precision.HIGHEST


def factor_inverse_kernel(scale, block, gram_ref, inverse_ref, work):
    count, rank, _ = gram_ref.shape
    lanes = lax.broadcasted_iota(jnp.int32, (rank, rank), 1)
    rows = lax.broadcasted_iota(jnp.int32, (rank, rank), 0)
    for m in range(count):
        work[m, :, :rank] = gram_ref[m] * scale
        work[m, :, rank:] = jnp.where(lanes == rows, 1.0, 0.0).astype(jnp.float32)
    small_rows = lax.broadcasted_iota(jnp.int32, (block, 2 * block), 0)
    small_lanes = lax.broadcasted_iota(jnp.int32, (block, 2 * block), 1)
    identity = jnp.where(small_rows + block == small_lanes, 1.0, 0.0).astype(jnp.float32)[:, block:]
    for step in range(rank // block):
        low = step * block
        heads = [
            jnp.concatenate([work[m, low : low + block, low : low + block], identity], axis=1)
            for m in range(count)
        ]
        scales = [jnp.zeros((block, 2 * block), jnp.float32) for _ in range(count)]
        for j in range(0, block, 2):
            for m in range(count):
                head = heads[m]
                left = jnp.broadcast_to(head[:, j : j + 1], head.shape)
                right = jnp.broadcast_to(head[:, j + 1 : j + 2], head.shape)
                pivot, cross = left[j : j + 1, :], left[j + 1 : j + 2, :]
                ratio = cross / pivot
                upper = head[j : j + 1, :] / pivot
                lower = head[j + 1 : j + 2, :] - ratio * head[j : j + 1, :]
                right = right - left * ratio
                second = right[j + 1 : j + 2, :]
                heads[m] = (
                    head - jnp.where(small_rows > j, left, 0.0) * upper
                    - jnp.where(small_rows > j + 1, right, 0.0) * (lower / second)
                )
                scales[m] = jnp.where(small_rows == j, lax.rsqrt(pivot), scales[m])
                scales[m] = jnp.where(small_rows == j + 1, lax.rsqrt(second), scales[m])
        for m in range(count):
            corner = (heads[m] * scales[m])[:, block:]
            panel = jnp.dot(corner, work[m, low : low + block, :], precision=HIGHEST, preferred_element_type=jnp.float32)
            work[m, low : low + block, :] = panel
            if low + block < rank:
                work[m, low + block :, :] -= lax.dot_general(
                    panel[:, low + block : rank], panel, (((0,), (0,)), ((), ())),
                    precision=HIGHEST, preferred_element_type=jnp.float32,
                )
    for m in range(count):
        inverse_ref[m] = jnp.where(lanes <= rows, work[m, :, rank:], 0.0)


def factor_inverse(gram_sum, total_rows):
    count, rank, _ = gram_sum.shape
    return pl.pallas_call(
        functools.partial(factor_inverse_kernel, 1.0 / total_rows, 32),
        out_shape=jax.ShapeDtypeStruct(gram_sum.shape, jnp.float32),
        in_specs=[pl.BlockSpec(memory_space=pltpu.VMEM)],
        out_specs=pl.BlockSpec(memory_space=pltpu.VMEM),
        scratch_shapes=[pltpu.VMEM((count, rank, 2 * rank), jnp.float32)],
        compiler_params=pltpu.CompilerParams(vmem_limit_bytes=16 << 20),
        cost_estimate=pl.CostEstimate(flops=20_000_000_000, bytes_accessed=2 << 20, transcendentals=0),
    )(gram_sum)


MESH = pl.DeviceIdType.MESH
SLOTS = 7
BLOCK = 256
TILE = 1024


def remote(source, target, send_sem, recv_sem, device):
    return pltpu.make_async_remote_copy(
        src_ref=source, dst_ref=target, send_sem=send_sem, recv_sem=recv_sem,
        device_id=device, device_id_type=MESH,
    )


def range_kernel(
    which, omega_ref, grad_ref, own_ref, gram_ref, keep_ref, give_ref, ring, total, parts,
    send_core, recv_core, send_chip, recv_chip, sums, grad_sem, send_sems, recv_sems,
):
    blocks = sums.shape[0]
    half_rows, rank = sums.shape[2:]
    row, col = lax.axis_index("row"), lax.axis_index("col")
    core = lax.rem(col, 2)
    sibling = (row, col + 1 - 2 * core)
    across = (row, lax.rem(col + 2, 4))

    def fetch(b):
        return pltpu.make_async_copy(
            grad_ref.at[which, pl.ds(b * BLOCK, BLOCK), :], ring.at[lax.rem(b, SLOTS)],
            grad_sem.at[lax.rem(b, SLOTS)],
        )

    def copy_partial(b):
        return remote(send_core.at[b], recv_core.at[b], send_sems.at[0, b], recv_sems.at[0, b], sibling)

    def copy_chip(b):
        return remote(send_chip.at[b], recv_chip.at[b], send_sems.at[1, b], recv_sems.at[1, b], across)

    def copy_sum(b):
        return remote(sums.at[b, core], sums.at[b, core], send_sems.at[2, b], recv_sems.at[2, b], sibling)

    for b in range(SLOTS):
        fetch(b).start()
    barrier = pltpu.get_barrier_semaphore()
    for peer in (sibling, across):
        pl.semaphore_signal(barrier, inc=1, device_id=peer, device_id_type=MESH)
    total[...] = jnp.zeros_like(total)
    gram_ref[...] = jnp.zeros_like(gram_ref)
    pl.semaphore_wait(barrier, 2)

    def step(s, carry):
        @pl.when(s < blocks)
        def _():
            fetch(s).wait()
            partial = jnp.dot(ring[lax.rem(s, SLOTS)], omega_ref[...], preferred_element_type=jnp.float32)
            parts[lax.rem(s, 2)] = partial.reshape(2, half_rows, rank)
            send_core[s] = parts[lax.rem(s, 2), 1 - core].astype(jnp.bfloat16)
            copy_partial(s).start()

        @pl.when((s >= 1) & (s < blocks + 1))
        def _():
            b = s - 1
            copy_partial(b).wait_recv()
            send_chip[b] = (parts[lax.rem(b, 2), core] + recv_core[b].astype(jnp.float32)).astype(jnp.bfloat16)
            copy_chip(b).start()

        @pl.when((s >= 3) & (s < blocks + 3))
        def _():
            b = s - 3
            copy_chip(b).wait_recv()
            sums[b, core] = (send_chip[b].astype(jnp.float32) + recv_chip[b].astype(jnp.float32)).astype(jnp.bfloat16)
            copy_sum(b).start()

        @pl.when(s >= 4)
        def _():
            b = s - 4
            copy_sum(b).wait_recv()
            block = sums[b].reshape(BLOCK, rank)
            turned = block.astype(jnp.float32).T.astype(jnp.bfloat16)
            gram_ref[...] += jnp.dot(turned, block, preferred_element_type=jnp.float32)
            slot = lax.rem(b, SLOTS)
            for low in range(0, total.shape[1], TILE):
                total[:, low : low + TILE] += jnp.dot(
                    turned, ring[slot, :, low : low + TILE], preferred_element_type=jnp.float32
                )

            @pl.when(b + SLOTS < blocks)
            def _():
                fetch(b + SLOTS).start()

        return carry

    lax.fori_loop(0, blocks + 4, step, 0)
    pairs, _, share = keep_ref.shape
    low = lax.rem(row, 2)
    for k in range(pairs):
        pair = 2 * lax.rem(row // 2 + k, pairs)
        keep_ref[k] = total[:, pl.ds(pl.multiple_of((pair + low) * share, share), share)].astype(jnp.bfloat16)
        give_ref[k] = total[:, pl.ds(pl.multiple_of((pair + 1 - low) * share, share), share)].astype(jnp.bfloat16)
    own = own_ref.shape[0]
    for i in range(own):
        own_ref[i] = sums[col * own + i].reshape(BLOCK, rank)

    def finish(b, carry):
        copy_partial(b).wait_send()
        copy_chip(b).wait_send()
        copy_sum(b).wait_send()
        return carry

    lax.fori_loop(0, blocks, finish, 0)


def sketch_and_moment(which, gradients, sketch_matrix, devices):
    _, rows, width = gradients.shape
    rank = sketch_matrix.shape[1]
    blocks = rows // BLOCK
    half = (blocks, BLOCK // 2, rank)
    vmem = pl.BlockSpec(memory_space=pltpu.VMEM)
    moment_half = jax.ShapeDtypeStruct((devices // 2, rank, width // devices), jnp.bfloat16)
    own, gram, keep, give = pl.pallas_call(
        functools.partial(range_kernel, which),
        out_shape=(
            jax.ShapeDtypeStruct((blocks // 4, BLOCK, rank), jnp.bfloat16),
            jax.ShapeDtypeStruct((rank, rank), jnp.float32),
            moment_half,
            moment_half,
        ),
        in_specs=[vmem, pl.BlockSpec(memory_space=pl.ANY)],
        out_specs=(vmem, vmem, vmem, vmem),
        scratch_shapes=[
            pltpu.VMEM((SLOTS, BLOCK, width), jnp.bfloat16),
            pltpu.VMEM((rank, width), jnp.float32),
            pltpu.VMEM((2, 2, BLOCK // 2, rank), jnp.float32),
            pltpu.VMEM(half, jnp.bfloat16),
            pltpu.VMEM(half, jnp.bfloat16),
            pltpu.VMEM(half, jnp.bfloat16),
            pltpu.VMEM(half, jnp.bfloat16),
            pltpu.VMEM((blocks, 2, BLOCK // 2, rank), jnp.bfloat16),
            pltpu.SemaphoreType.DMA((SLOTS,)),
            pltpu.SemaphoreType.DMA((3, blocks)),
            pltpu.SemaphoreType.DMA((3, blocks)),
        ],
        compiler_params=pltpu.CompilerParams(
            collective_id=which, has_side_effects=True, vmem_limit_bytes=44 << 20
        ),
        cost_estimate=pl.CostEstimate(
            flops=4 * rows * width * rank, bytes_accessed=2 * rows * width, transcendentals=0
        ),
    )(sketch_matrix, gradients)
    return own.reshape(rows // 4, rank), gram, keep, give


def gram_kernel(gram_ref, sum_ref, landed, row_send, row_recv, out_send, out_recv, col_send, col_recv):
    count, piece, _ = landed.shape
    row, col = lax.axis_index("row"), lax.axis_index("col")
    cols = lax.axis_size("col")
    quarter = count * piece
    base = col * quarter
    rows_of = lambda r: pl.ds(pl.multiple_of(base + r * piece, piece), piece)
    row_peers = [(lax.rem(row + k, count), col) for k in range(1, count)]
    col_peers = [(row, lax.rem(col + k, cols)) for k in range(1, cols)]
    barrier = pltpu.get_barrier_semaphore()
    for peer in row_peers + col_peers:
        pl.semaphore_signal(barrier, inc=1, device_id=peer, device_id_type=MESH)
    pl.semaphore_wait(barrier, count + cols - 2)

    first = [
        remote(gram_ref.at[rows_of(peer[0])], landed.at[k], row_send.at[k], row_recv.at[k], peer)
        for k, peer in enumerate(row_peers)
    ]
    for copy in first:
        copy.start()
    here = gram_ref[rows_of(row)]
    for k, copy in enumerate(first):
        copy.wait_recv()
        here += landed[k]
    sum_ref[rows_of(row)] = here
    second = [
        remote(sum_ref.at[rows_of(row)], sum_ref.at[rows_of(row)], out_send.at[k], out_recv.at[k], peer)
        for k, peer in enumerate(row_peers)
    ]
    for copy in second:
        copy.start()
    for copy in second:
        copy.wait_recv()
    mine = pl.ds(pl.multiple_of(base, quarter), quarter)
    third = [
        remote(sum_ref.at[mine], sum_ref.at[mine], col_send.at[k], col_recv.at[k], peer)
        for k, peer in enumerate(col_peers)
    ]
    for copy in third:
        copy.start()
    for copy in third:
        copy.wait_recv()
    for copy in first + second + third:
        copy.wait_send()


def add_grams(gram, rows, cols):
    lines, rank = gram.shape
    piece = lines // (rows * cols)
    vmem = pl.BlockSpec(memory_space=pltpu.VMEM)
    return pl.pallas_call(
        gram_kernel,
        out_shape=jax.ShapeDtypeStruct(gram.shape, jnp.float32),
        in_specs=[vmem],
        out_specs=vmem,
        scratch_shapes=[pltpu.VMEM((rows, piece, rank), jnp.float32)]
        + [pltpu.SemaphoreType.DMA((rows - 1,))] * 4
        + [pltpu.SemaphoreType.DMA((cols - 1,))] * 2,
        compiler_params=pltpu.CompilerParams(
            collective_id=2, has_side_effects=True, vmem_limit_bytes=8 << 20
        ),
        cost_estimate=pl.CostEstimate(flops=20_000_000_000, bytes_accessed=2 << 20, transcendentals=0),
    )(gram)


def finish_outputs(mine, gram_sum, moments, total_rows):
    inverse_low = factor_inverse(gram_sum, total_rows)
    inverse_low, moments = lax.optimization_barrier((inverse_low, moments))
    projector = jnp.einsum(
        "mrk,mlk->mrl", mine.astype(jnp.float32), inverse_low, precision=HIGHEST
    ).astype(jnp.bfloat16)
    scaled = inverse_low * (1.0 / math.sqrt(total_rows))
    part = jnp.stack(
        [jnp.dot(scaled[m], moments[m].astype(jnp.float32), precision=HIGHEST) for m in range(2)], 1
    ).astype(jnp.bfloat16)
    projected = lax.all_to_all(part, "row", split_axis=0, concat_axis=2, tiled=True).astype(jnp.float32)
    return (projector, projected)


def add_pairs(keep, give, devices):
    got = lax.ppermute(give, "row", [(r, r + 1 - 2 * (r % 2)) for r in range(devices)])
    paired = keep.astype(jnp.float32) + got.astype(jnp.float32)
    return paired[0], [paired[k].astype(jnp.bfloat16) for k in range(1, devices // 2)]


def add_moments(first, others, devices):
    moment = first
    for k, other in enumerate(others, 1):
        ring = [(r, (r + 2 * k) % devices) for r in range(devices)]
        moment += lax.ppermute(other, "row", ring).astype(jnp.float32)
    return moment


def body_fused(gradients, sketch_matrix):
    rows, cols = lax.axis_size("row"), lax.axis_size("col")
    mine, grams, pairs = [], [], []
    for m in range(2):
        own, gram, keep, give = sketch_and_moment(m, gradients, sketch_matrix, rows)
        mine.append(own)
        grams.append(gram)
        pairs.append(add_pairs(keep, give, rows))
    rank = sketch_matrix.shape[1]
    grams, pairs[0] = lax.optimization_barrier((grams, pairs[0]))
    moment = add_moments(*pairs[0], rows)
    gram_sum = add_grams(jnp.concatenate(grams, 0), rows, cols)
    gram_sum, moment, pairs[1] = lax.optimization_barrier((gram_sum, moment, pairs[1]))
    moments = [moment, add_moments(*pairs[1], rows)]
    return finish_outputs(jnp.stack(mine), gram_sum.reshape(2, rank, rank), moments, gradients.shape[1] * rows)


def body_plain(gradients, sketch_matrix):
    total_rows = gradients.shape[1] * lax.axis_size("row")
    partial_sketch = jnp.einsum(
        "mrd,dk->mrk", gradients, sketch_matrix, preferred_element_type=jnp.float32
    ).astype(jnp.bfloat16)
    mine = lax.psum_scatter(partial_sketch, "col", scatter_dimension=1, tiled=True)
    sketch_rows = lax.all_gather(mine, "col", axis=1, tiled=True)
    local_gram = jnp.einsum("mrk,mrl->mkl", mine, mine, preferred_element_type=jnp.float32)
    gram_sum = lax.psum(local_gram, ("row", "col"))
    moments = []
    for m in range(2):
        moment = jnp.einsum("rk,rd->kd", sketch_rows[m], gradients[m], preferred_element_type=jnp.float32)
        moments.append(lax.psum_scatter(moment.astype(jnp.bfloat16), "row", scatter_dimension=1, tiled=True))
    return finish_outputs(mine, gram_sum, moments, total_rows)


def solution(mesh):
    in_specs = (P(None, "row", "col"), P("col", None))
    out_specs = (P(None, ("row", "col"), None), P("row", None, "col"))

    def body(gradients, sketch_matrix):
        _, rows, width = gradients.shape
        rank = sketch_matrix.shape[1]
        fits = mesh.shape["col"] == 4 and mesh.shape["row"] % 2 == 0 and rows % (4 * BLOCK) == 0 and rows >= SLOTS * BLOCK and width % TILE == 0 and width % (128 * mesh.shape["row"]) == 0
        fits = fits and (2 * rank) % (16 * mesh.shape["row"] * mesh.shape["col"]) == 0
        return (body_fused if fits else body_plain)(gradients, sketch_matrix)

    return jax.shard_map(body, mesh=mesh, in_specs=in_specs, out_specs=out_specs, check_vma=False)
```
